32 devices in a mesh: pipe: 4 (over y, x), ctx: 8 (over z, core).
Axes of the slice: x: 2, y: 2, z: 4, core: 2. Of those that a mesh axis runs over, the one named last changes fastest.
Arguments:
- features: bfloat16 [4, 1024, 12288], P('pipe', 'ctx'), may hold values from -6 to 6
- short_taps: float32 [4, 3, 12288], P('pipe'), may hold values from -3.5 to 3.5
- decays: float32 [4, 4096, 16], P('pipe'), may hold values from 0.00048828125 to 0.04
- residues: float32 [4, 4096, 16], P('pipe'), may hold values from -1.5 to 1.5
- skip_gain: float32 [4, 4096], P('pipe'), may hold values from -3 to 3
Outputs:
- received: bfloat16 [4, 1024, 4096], P('pipe', 'ctx')
The draws below stay inside these ranges and needn't reach their ends.
All inputs are finite; a program needn't handle non-finite values.
Results may differ from the reference program's by a relative error of at most 0.0058.
Values may be sent and summed in bfloat16 or wider, within the bound.
A program may use at most 64 MiB of HBM per device.

```python
import math
import jax
import jax.numpy as jnp
from jax import lax

C = 4096
ORDER = 16
KERNEL = 3
FEAT = 12288
SEQ = 1024
SECTIONS = 4


def block_levels(key, extent, split, least, top_value):
    factor_of, own = 1.0, jax.random.fold_in(key, 6)
    for dim, shards_of in split:
        heights = jnp.exp(jax.random.uniform(jax.random.fold_in(own, dim), (shards_of,), jnp.float32, least / len(split), top_value / len(split)))
        factor_of = factor_of * jnp.repeat(heights, extent[dim] // shards_of).reshape([-1 if axis == dim else 1 for axis in range(len(extent))])
    return factor_of


def scatter_about(own_key, extent, scale, limit, cuts=(), kind=jnp.bfloat16):
    array = scale * jax.random.normal(own_key, extent, jnp.float32)
    if cuts:
        array = array * block_levels(own_key, extent, cuts, -0.22, 0.18)
    return jnp.clip(array, -limit, limit).astype(kind)


def setup_inputs(seed: int = 0) -> dict:
    keys = jax.random.split(jax.random.key(seed), 6)
    features = scatter_about(keys[0], (SECTIONS, SEQ, FEAT), 1.0, 6.0, ((0, 4), (1, 8)))
    short_taps = scatter_about(keys[1], (SECTIONS, KERNEL, FEAT), KERNEL ** -0.5, 3.5, ((0, 4),), jnp.float32)
    decays = jnp.clip(jnp.exp(math.log(0.04) - 4.405743 * jax.random.uniform(keys[2], (SECTIONS, C, ORDER), jnp.float32) ** block_levels(keys[2], (SECTIONS, C, ORDER), ((0, 4),), -0.2, 0.2)), 0.00048828125, 0.04)
    residues = scatter_about(keys[3], (SECTIONS, C, ORDER), 0.25, 1.5, ((0, 4),), jnp.float32)
    skip_gain = scatter_about(keys[4], (SECTIONS, C), 0.5, 3.0, ((0, 4),), jnp.float32)
    return dict(features=features, short_taps=short_taps, decays=decays, residues=residues, skip_gain=skip_gain)


def modal_conv(signal, decay_rate, residue_set):
    length, channels = signal.shape
    block_len = math.gcd(length, 128)
    nblocks = length // block_len
    weight = residue_set * jnp.sqrt(decay_rate)
    offsets = jnp.arange(block_len, dtype=jnp.float32)
    falling = jnp.exp(-decay_rate[:, :, None] * offsets)
    rising = jnp.exp(decay_rate[:, :, None] * offsets)
    head_w = weight[:, :, None] * falling
    blocks = signal.reshape(nblocks, block_len, channels)
    lower = (jnp.arange(block_len)[:, None] >= jnp.arange(block_len)[None, :]).astype(jnp.float32)
    scaled = blocks[:, :, :, None] * jnp.transpose(rising, (2, 0, 1))[None]
    prefix = jnp.einsum('ij,bjcn->bicn', lower, scaled, precision=lax.Precision.HIGHEST)
    inside = jnp.einsum('cni,bicn->bic', head_w, prefix, precision=lax.Precision.HIGHEST)
    tail_w = jnp.exp(-decay_rate[:, :, None] * (block_len - offsets))
    block_ends = jnp.einsum('cnj,bjc->bcn', tail_w, blocks, precision=lax.Precision.HIGHEST)
    stride = jnp.exp(-decay_rate * block_len)

    def advance(carry_state, finish):
        return (carry_state * stride + finish, carry_state)
    final_state, starts = lax.scan(advance, jnp.zeros(decay_rate.shape, jnp.float32), block_ends)
    carried = jnp.einsum('cni,bcn->bic', head_w, starts, precision=lax.Precision.HIGHEST)
    return ((inside + carried).reshape(length, channels), final_state)

def short_conv(padded, taps_now, row_count):
    kernel_len = taps_now.shape[0]
    summed = jnp.zeros((row_count, padded.shape[1]), jnp.float32)
    for shift_by in range(kernel_len):
        offset_row = kernel_len - 1 - shift_by
        summed = summed + taps_now[shift_by] * padded[offset_row:offset_row + row_count].astype(jnp.float32)
    return summed

def conv_group(bundle):
    return modal_conv(bundle[0], bundle[1], bundle[2])

def run_section(bundle):
    inputs, taps_now, decay_now, residue_now, skip_now = bundle
    row_total = inputs.shape[0]
    channels = inputs.shape[1] // 3
    kernel_len = taps_now.shape[0]
    padded = jnp.concatenate([jnp.zeros((kernel_len - 1, inputs.shape[1]), jnp.bfloat16), inputs], axis=0)
    filtered = short_conv(padded, taps_now, row_total)
    queries = filtered[:, :channels]
    key_value = (filtered[:, channels:2 * channels] * filtered[:, 2 * channels:]).astype(jnp.bfloat16)
    signal = lax.optimization_barrier(key_value).astype(jnp.float32)
    group = math.gcd(channels, 128)
    ngroups = channels // group
    grouped = signal.reshape(row_total, ngroups, group).transpose(1, 0, 2)
    decay_groups = decay_now.reshape(ngroups, group, decay_now.shape[1])
    residue_groups = residue_now.reshape(ngroups, group, residue_now.shape[1])
    outputs, finals = lax.map(conv_group, (grouped, decay_groups, residue_groups))
    conv = outputs.transpose(1, 0, 2).reshape(row_total, channels) + skip_now * signal
    mixed = lax.optimization_barrier(conv.astype(jnp.bfloat16)).astype(jnp.float32)
    return (queries * mixed).astype(jnp.bfloat16)

def reference(features, short_taps, decays, residues, skip_gain):
    gated = lax.map(run_section, (features, short_taps, decays, residues, skip_gain))
    return jnp.roll(gated, 1, axis=0)
```

```python
import functools

import jax
import jax.numpy as jnp
from jax import lax
from jax.experimental import pallas as pl
from jax.experimental.pallas import tpu as pltpu
from jax.sharding import PartitionSpec as P

LANES = 128
SUBS = 8
MESH = pl.DeviceIdType.MESH


def lanes_of(group):
    return pl.ds(pl.multiple_of(group * LANES, LANES), LANES)


def mixer_kernel(
    n,
    stages,
    feat,
    taps,
    dec,
    res,
    skip,
    out,
    fv,
    tail,
    halo_s,
    halo_r,
    pad,
    kv,
    rate,
    amp,
    sub_state,
    conv,
    ends,
    ends_r,
    starts,
    starts_r,
    gate,
    load_sem,
    halo_send,
    halo_recv,
    ends_send,
    ends_recv,
    starts_send,
    starts_recv,
    gate_send,
    gate_recv,
):
    rows, width = fv.shape
    channels = width // 3
    groups = channels // LANES
    per = groups // n
    order = dec.shape[2]
    sub = rows // SUBS
    me = lax.axis_index("ctx")
    stage = lax.axis_index("pipe")
    later = lax.rem(stage + 1, stages)
    before = lax.rem(stage + stages - 1, stages)

    tail_load = pltpu.make_async_copy(feat.at[0, pl.ds(rows - 16, 16)], tail, load_sem.at[0])
    kv_load = pltpu.make_async_copy(
        feat.at[0, :, pl.ds(channels, 2 * channels)],
        fv.at[:, pl.ds(channels, 2 * channels)],
        load_sem.at[1],
    )
    query_load = pltpu.make_async_copy(
        feat.at[0, :, pl.ds(0, channels)], fv.at[:, pl.ds(0, channels)], load_sem.at[2]
    )
    tail_load.start()
    kv_load.start()
    query_load.start()

    barrier = pltpu.get_barrier_semaphore()
    for other in (later, before):
        pl.semaphore_signal(barrier, inc=1, device_id={"pipe": other}, device_id_type=MESH)
    for step in range(1, n):
        other = lax.rem(me + step, n)
        pl.semaphore_signal(barrier, inc=1, device_id={"ctx": other}, device_id_type=MESH)

    tail_load.wait()

    @pl.loop(0, width // LANES)
    def _(group):
        at = lanes_of(group)
        halo_s[:, at] = tail[:, at].astype(jnp.float32)[14:16]

    pl.semaphore_wait(barrier, n + 1)

    halo_copy = pltpu.make_async_remote_copy(
        src_ref=halo_s,
        dst_ref=halo_r,
        send_sem=halo_send,
        recv_sem=halo_recv,
        device_id={"ctx": lax.rem(me + 1, n)},
        device_id_type=MESH,
    )

    @pl.when(me < n - 1)
    def _():
        halo_copy.start()

    @pl.when(me == 0)
    def _():
        halo_r[...] = jnp.zeros_like(halo_r)

    @pl.when(me > 0)
    def _():
        halo_copy.wait_recv()

    kv_load.wait()

    place = lax.broadcasted_iota(jnp.int32, (SUBS, LANES), 0)
    place_f = place.astype(jnp.float32)

    def filtered(group, slot):
        at = lanes_of(group)
        now = fv[:, at].astype(jnp.float32)
        pad[slot, pl.ds(6, 2), :] = halo_r[:, at]
        pad[slot, pl.ds(8, rows), :] = now
        tap = taps[0, :, at]
        total = tap[0:1] * now
        for shift in range(1, 3):
            total = total + tap[shift : shift + 1] * pad[slot, pl.ds(8 - shift, rows), :]
        return total

    def spread(row):
        return jnp.broadcast_to(row, (SUBS, LANES))

    def first_pass(group):
        keys = filtered(groups + group, 0)
        values = filtered(2 * groups + group, 1)
        kv[group] = (keys * values).astype(jnp.bfloat16).astype(jnp.float32)
        mine = pl.ds(pl.multiple_of(group * LANES, LANES), LANES)
        a = jnp.transpose(dec[0, mine, :])
        r = jnp.transpose(res[0, mine, :])
        rate[group] = a
        amp[group] = r * jnp.sqrt(a)
        one = jnp.exp(-a)
        jumps = [jnp.exp(-a * float(sub * hop)) for hop in (1, 2, 4)]
        signal = [kv[group, pl.ds(j, SUBS, stride=sub), :] for j in range(sub)]
        for m in range(order):
            lam = spread(one[m : m + 1])
            state = signal[0]
            for j in range(1, sub):
                state = state * lam + signal[j]
            for hop, jump in zip((1, 2, 4), jumps):
                factor = jnp.where(place >= hop, spread(jump[m : m + 1]), 0.0)
                state = state + factor * pltpu.roll(state, hop, 0)
            sub_state[group, m] = state
            ends[group, m : m + 1, :] = state[SUBS - 1 : SUBS]

    def ends_copy(owner, slot):
        return pltpu.make_async_remote_copy(
            src_ref=ends.at[pl.ds(owner * per, per)],
            dst_ref=ends_r.at[slot],
            send_sem=ends_send.at[owner],
            recv_sem=ends_recv.at[slot],
            device_id={"ctx": owner},
            device_id_type=MESH,
        )

    def starts_copy(target, slot):
        return pltpu.make_async_remote_copy(
            src_ref=starts.at[target],
            dst_ref=starts_r.at[slot],
            send_sem=starts_send.at[target],
            recv_sem=starts_recv.at[slot],
            device_id={"ctx": target},
            device_id_type=MESH,
        )

    def gate_copy(chunk):
        at = pl.ds(pl.multiple_of(chunk * (per * LANES), LANES), per * LANES)
        return pltpu.make_async_remote_copy(
            src_ref=gate.at[:, at],
            dst_ref=out.at[0, :, at],
            send_sem=gate_send.at[chunk],
            recv_sem=gate_recv.at[chunk],
            device_id={"pipe": later},
            device_id_type=MESH,
        )

    @pl.loop(1, n + 1)
    def _(step):
        owner = lax.rem(me + step, n)

        @pl.loop(0, per)
        def _(k):
            first_pass(owner * per + k)

        @pl.when(step < n)
        def _():
            ends_copy(owner, me).start()

    ends_r[me] = ends[pl.ds(me * per, per)]

    @pl.loop(1, n)
    def _(step):
        ends_copy(lax.rem(me + step, n), lax.rem(me + step, n)).wait_recv()

    @pl.loop(0, per)
    def _(k):
        across = jnp.exp(-rate[me * per + k] * float(rows))

        def advance(i, state):
            starts[i, k] = state
            return state * across + ends_r[i, k]

        lax.fori_loop(0, n, advance, jnp.zeros((order, LANES), jnp.float32))

    starts_r[me] = starts[me]

    @pl.loop(1, n)
    def _(step):
        starts_copy(lax.rem(me + step, n), me).start()

    query_load.wait()

    def second_pass(chunk, k):
        group = chunk * per + k
        entering = starts_r[chunk, k]
        a = rate[group]
        w = amp[group]
        one = jnp.exp(-a)
        lam = [spread(one[m : m + 1]) for m in range(order)]
        state = []
        for m in range(order):
            decayed = jnp.exp(-spread(a[m : m + 1]) * (place_f * float(sub)))
            inner = jnp.where(place >= 1, pltpu.roll(sub_state[group, m], 1, 0), 0.0)
            state.append(inner + decayed * spread(entering[m : m + 1]))
        gain = skip[:, lanes_of(group)]
        for j in range(sub):
            now = kv[group, pl.ds(j, SUBS, stride=sub), :]
            parts = [gain * now, None]
            for m in range(order):
                state[m] = state[m] * lam[m] + now
                term = spread(w[m : m + 1]) * state[m]
                parts[m % 2] = term if parts[m % 2] is None else parts[m % 2] + term
            conv[pl.ds(j, SUBS, stride=sub), :] = parts[0] + parts[1]
        mixed = conv[...].astype(jnp.bfloat16).astype(jnp.float32)
        queries = filtered(group, 2)
        gate[:, lanes_of(group)] = (queries * mixed).astype(jnp.bfloat16)

    @pl.loop(0, n)
    def _(step):
        chunk = lax.rem(me + step, n)

        @pl.when(step > 0)
        def _():
            starts_copy(chunk, chunk).wait_recv()

        @pl.loop(0, per)
        def _(k):
            second_pass(chunk, k)

        gate_copy(chunk).start()

    @pl.when(me < n - 1)
    def _():
        halo_copy.wait_send()

    @pl.loop(1, n)
    def _(step):
        other = lax.rem(me + step, n)
        ends_copy(other, me).wait_send()
        starts_copy(other, me).wait_send()

    @pl.loop(0, n)
    def _(chunk):
        copy = gate_copy(chunk)
        copy.wait_send()
        copy.wait_recv()


def local(n, stages, features, short_taps, decays, residues, skip_gain):
    rows, width = features.shape[1:]
    channels = width // 3
    order = decays.shape[2]
    groups = channels // LANES
    per = groups // n
    f32 = jnp.float32
    vmem = pl.BlockSpec(memory_space=pltpu.VMEM)
    hbm = pl.BlockSpec(memory_space=pl.ANY)
    return pl.pallas_call(
        functools.partial(mixer_kernel, n, stages),
        out_shape=jax.ShapeDtypeStruct((1, rows, channels), jnp.bfloat16),
        in_specs=[hbm, vmem, vmem, vmem, vmem],
        out_specs=hbm,
        scratch_shapes=[
            pltpu.VMEM((rows, width), jnp.bfloat16),
            pltpu.VMEM((16, width), jnp.bfloat16),
            pltpu.VMEM((2, width), f32),
            pltpu.VMEM((2, width), f32),
            pltpu.VMEM((3, rows + 8, LANES), f32),
            pltpu.VMEM((groups, rows, LANES), f32),
            pltpu.VMEM((groups, order, LANES), f32),
            pltpu.VMEM((groups, order, LANES), f32),
            pltpu.VMEM((groups, order, SUBS, LANES), f32),
            pltpu.VMEM((rows, LANES), f32),
            pltpu.VMEM((groups, order, LANES), f32),
            pltpu.VMEM((n, per, order, LANES), f32),
            pltpu.VMEM((n, per, order, LANES), f32),
            pltpu.VMEM((n, per, order, LANES), f32),
            pltpu.VMEM((rows, channels), jnp.bfloat16),
            pltpu.SemaphoreType.DMA((3,)),
            pltpu.SemaphoreType.DMA,
            pltpu.SemaphoreType.DMA,
            pltpu.SemaphoreType.DMA((n,)),
            pltpu.SemaphoreType.DMA((n,)),
            pltpu.SemaphoreType.DMA((n,)),
            pltpu.SemaphoreType.DMA((n,)),
            pltpu.SemaphoreType.DMA((n,)),
            pltpu.SemaphoreType.DMA((n,)),
        ],
        compiler_params=pltpu.CompilerParams(
            collective_id=0, has_side_effects=True, vmem_limit_bytes=40 * 1024 * 1024
        ),
        name="mixer",
    )(features, short_taps, decays, residues, skip_gain)


def solution(mesh):
    in_specs = (
        P("pipe", "ctx", None),
        P("pipe", None, None),
        P("pipe", None, None),
        P("pipe", None, None),
        P("pipe", None),
    )
    out_specs = P("pipe", "ctx", None)
    body = functools.partial(local, mesh.shape["ctx"], mesh.shape["pipe"])
    return jax.shard_map(body, mesh=mesh, in_specs=in_specs, out_specs=out_specs, check_vma=False)
```

```python
import functools

import jax
import jax.numpy as jnp
from jax import lax
from jax.experimental import pallas as pl
from jax.experimental.pallas import tpu as pltpu
from jax.sharding import PartitionSpec as P

LANES = 128
SUBS = 8
MESH = pl.DeviceIdType.MESH


def lanes_of(group):
    return pl.ds(pl.multiple_of(group * LANES, LANES), LANES)


def mixer_kernel(
    n,
    stages,
    feat,
    taps_h,
    dec_h,
    res_h,
    skip_h,
    out,
    taps,
    dec,
    res,
    skip,
    fv,
    tail,
    halo_s,
    halo_r,
    pad,
    kv,
    drift,
    amp,
    sub_state,
    conv,
    ends,
    ends_r,
    starts,
    starts_r,
    gate,
    load_sem,
    halo_send,
    halo_recv,
    ends_send,
    ends_recv,
    starts_send,
    starts_recv,
    gate_send,
    gate_recv,
):
    rows, width = fv.shape
    channels = width // 3
    groups = channels // LANES
    per = groups // n
    order = dec.shape[0]
    sub = rows // SUBS
    me = lax.axis_index("ctx")
    stage = lax.axis_index("pipe")
    later = lax.rem(stage + 1, stages)
    before = lax.rem(stage + stages - 1, stages)

    tail_load = pltpu.make_async_copy(feat.at[0, pl.ds(rows - 16, 16)], tail, load_sem.at[0])
    kv_load = pltpu.make_async_copy(
        feat.at[0, :, pl.ds(channels, 2 * channels)],
        fv.at[:, pl.ds(channels, 2 * channels)],
        load_sem.at[1],
    )
    query_load = pltpu.make_async_copy(
        feat.at[0, :, pl.ds(0, channels)], fv.at[:, pl.ds(0, channels)], load_sem.at[2]
    )
    small_loads = [
        pltpu.make_async_copy(source, target, load_sem.at[3 + i])
        for i, (source, target) in enumerate(
            ((taps_h, taps), (dec_h, dec), (res_h, res), (skip_h, skip))
        )
    ]
    tail_load.start()
    for load in small_loads:
        load.start()
    kv_load.start()
    query_load.start()

    barrier = pltpu.get_barrier_semaphore()
    for other in (later, before):
        pl.semaphore_signal(barrier, inc=1, device_id={"pipe": other}, device_id_type=MESH)
    for step in range(1, n):
        other = lax.rem(me + step, n)
        pl.semaphore_signal(barrier, inc=1, device_id={"ctx": other}, device_id_type=MESH)

    pad[0, pl.ds(0, 8), :] = jnp.zeros((8, LANES), jnp.float32)
    pad[1, pl.ds(0, 8), :] = jnp.zeros((8, LANES), jnp.float32)
    tail_load.wait()

    @pl.loop(0, width // LANES, unroll=8)
    def _(group):
        at = lanes_of(group)
        halo_s[:, at] = tail[:, at].astype(jnp.float32)[14:16]

    pl.semaphore_wait(barrier, n + 1)

    halo_copy = pltpu.make_async_remote_copy(
        src_ref=halo_s,
        dst_ref=halo_r,
        send_sem=halo_send,
        recv_sem=halo_recv,
        device_id={"ctx": lax.rem(me + 1, n)},
        device_id_type=MESH,
    )

    @pl.when(me < n - 1)
    def _():
        halo_copy.start()

    @pl.when(me == 0)
    def _():
        halo_r[...] = jnp.zeros_like(halo_r)

    for load in small_loads:
        load.wait()
    kv_load.wait()

    place = lax.broadcasted_iota(jnp.int32, (SUBS, LANES), 0)
    place_f = place.astype(jnp.float32)

    def filtered(group, slot, now, count):
        at = lanes_of(group)
        pad[slot, pl.ds(8, count), :] = now
        total = taps[0, :, at] * now
        for shift in range(1, 3):
            total = total + taps[shift, :, at] * pad[slot, pl.ds(8 - shift, count), :]
        return total

    def filtered_whole(group, slot):
        return filtered(group, slot, fv[:, lanes_of(group)].astype(jnp.float32), rows)

    def filtered_head(group, slot):
        at = lanes_of(group)
        pad[slot, pl.ds(6, 2), :] = halo_r[:, at]
        return filtered(group, slot, fv[pl.ds(0, 16), at].astype(jnp.float32)[0:8], 8)

    def rounded(product):
        return product.astype(jnp.bfloat16).astype(jnp.float32)

    def spread(row):
        return jnp.broadcast_to(row, (SUBS, LANES))

    def first_pass(group):
        keys = filtered_whole(groups + group, 0)
        values = filtered_whole(2 * groups + group, 1)
        kv[group] = rounded(keys * values)
        a = dec[:, lanes_of(group)]
        amp[group] = res[:, lanes_of(group)] * jnp.sqrt(a)
        one = jnp.exp(-a)
        jumps = [jnp.exp(-a * float(sub * hop)) for hop in (1, 2, 4)]
        signal = [kv[group, pl.ds(j, SUBS, stride=sub), :] for j in range(sub)]
        for m in range(order):
            lam = spread(one[m : m + 1])
            state = signal[0]
            for j in range(1, sub):
                state = state * lam + signal[j]
            for hop, jump in zip((1, 2, 4), jumps):
                factor = jnp.where(place >= hop, spread(jump[m : m + 1]), 0.0)
                state = state + factor * pltpu.roll(state, hop, 0)
            sub_state[group, m] = state
            ends[group, m : m + 1, :] = state[SUBS - 1 : SUBS]

    def join_halo(group):
        product = filtered_head(groups + group, 3) * filtered_head(2 * groups + group, 4)
        true = rounded(product)
        delta = true - kv[group, pl.ds(0, 8), :]
        kv[group, pl.ds(0, 8), :] = true
        a = dec[:, lanes_of(group)]
        extra = jnp.exp(a) * delta[0:1] + jnp.exp(2.0 * a) * delta[1:2]
        drift[group] = extra
        ends[group] = ends[group] + jnp.exp(-a * float(rows)) * extra

    def ends_copy(turn, owner, slot):
        return pltpu.make_async_remote_copy(
            src_ref=ends.at[owner * per + turn],
            dst_ref=ends_r.at[turn, slot],
            send_sem=ends_send.at[turn, owner],
            recv_sem=ends_recv.at[turn, slot],
            device_id={"ctx": owner},
            device_id_type=MESH,
        )

    def starts_copy(turn, target, slot):
        return pltpu.make_async_remote_copy(
            src_ref=starts.at[turn, target],
            dst_ref=starts_r.at[turn, slot],
            send_sem=starts_send.at[turn, target],
            recv_sem=starts_recv.at[turn, slot],
            device_id={"ctx": target},
            device_id_type=MESH,
        )

    def gate_copy(group):
        at = lanes_of(group)
        return pltpu.make_async_remote_copy(
            src_ref=gate.at[:, at],
            dst_ref=out.at[0, :, at],
            send_sem=gate_send.at[group],
            recv_sem=gate_recv.at[group],
            device_id={"pipe": later},
            device_id_type=MESH,
        )

    def second_pass(turn, chunk):
        group = chunk * per + turn
        entering = starts_r[turn, chunk]
        a = dec[:, lanes_of(group)]
        w = amp[group]
        one = jnp.exp(-a)
        joined = entering + drift[group]
        lam = [spread(one[m : m + 1]) for m in range(order)]
        state = []
        for m in range(order):
            decayed = jnp.exp(-spread(a[m : m + 1]) * (place_f * float(sub)))
            inner = pltpu.roll(sub_state[group, m], 1, 0) + decayed * spread(joined[m : m + 1])
            state.append(jnp.where(place >= 1, inner, spread(entering[m : m + 1])))
        gain = skip[:, lanes_of(group)]
        for j in range(sub):
            now = kv[group, pl.ds(j, SUBS, stride=sub), :]
            parts = [gain * now, None]
            for m in range(order):
                state[m] = state[m] * lam[m] + now
                term = spread(w[m : m + 1]) * state[m]
                parts[m % 2] = term if parts[m % 2] is None else parts[m % 2] + term
            conv[pl.ds(j, SUBS, stride=sub), :] = parts[0] + parts[1]
        mixed = rounded(conv[...])
        pad[2, pl.ds(6, 2), :] = halo_r[:, lanes_of(group)]
        queries = filtered_whole(group, 2)
        gate[:, lanes_of(group)] = (queries * mixed).astype(jnp.bfloat16)

    def collect(turn):
        @pl.loop(1, n + 1)
        def _(step):
            first_pass(lax.rem(me + step, n) * per + turn)

        @pl.when((turn == 0) & (me > 0))
        def _():
            halo_copy.wait_recv()

        @pl.loop(1, n + 1)
        def _(step):
            owner = lax.rem(me + step, n)
            join_halo(owner * per + turn)

            @pl.when(step < n)
            def _():
                ends_copy(turn, owner, me).start()

        ends_r[turn, me] = ends[me * per + turn]

    def scan(turn):
        @pl.loop(1, n)
        def _(step):
            other = lax.rem(me + step, n)
            ends_copy(turn, other, other).wait_recv()

        across = jnp.exp(-dec[:, lanes_of(me * per + turn)] * float(rows))

        def advance(i, state):
            starts[turn, i] = state
            return state * across + ends_r[turn, i]

        lax.fori_loop(0, n, advance, jnp.zeros((order, LANES), jnp.float32))
        starts_r[turn, me] = starts[turn, me]

        @pl.loop(1, n)
        def _(step):
            starts_copy(turn, lax.rem(me + step, n), me).start()

    def produce(turn):
        @pl.when(turn == 0)
        def _():
            query_load.wait()

        @pl.loop(0, n)
        def _(step):
            chunk = lax.rem(me + step, n)

            @pl.when(step > 0)
            def _():
                starts_copy(turn, chunk, chunk).wait_recv()

            second_pass(turn, chunk)
            gate_copy(chunk * per + turn).start()

    @pl.loop(0, per + 2)
    def _(phase):
        @pl.when(phase < per)
        def _():
            collect(phase)

        @pl.when((phase >= 1) & (phase <= per))
        def _():
            scan(phase - 1)

        @pl.when(phase >= 2)
        def _():
            produce(phase - 2)

    @pl.when(me < n - 1)
    def _():
        halo_copy.wait_send()

    @pl.loop(0, per)
    def _(turn):
        @pl.loop(1, n)
        def _(step):
            other = lax.rem(me + step, n)
            ends_copy(turn, other, me).wait_send()
            starts_copy(turn, other, me).wait_send()

    @pl.loop(0, groups)
    def _(group):
        copy = gate_copy(group)
        copy.wait_send()
        copy.wait_recv()


def local(n, stages, features, short_taps, decays, residues, skip_gain):
    rows, width = features.shape[1:]
    channels = width // 3
    order = decays.shape[2]
    groups = channels // LANES
    per = groups // n
    f32 = jnp.float32
    hbm = pl.BlockSpec(memory_space=pltpu.HBM)
    where = pl.BlockSpec(memory_space=pl.ANY)
    bf16 = jnp.bfloat16
    copies = pltpu.SemaphoreType.DMA
    return pl.pallas_call(
        functools.partial(mixer_kernel, n, stages),
        out_shape=jax.ShapeDtypeStruct((1, rows, channels), jnp.bfloat16),
        in_specs=[hbm] * 5,
        out_specs=where,
        scratch_shapes=[
            pltpu.VMEM((3, 1, width), f32),
            pltpu.VMEM((order, channels), f32),
            pltpu.VMEM((order, channels), f32),
            pltpu.VMEM((1, channels), f32),
            pltpu.VMEM((rows, width), bf16),
            pltpu.VMEM((16, width), bf16),
            pltpu.VMEM((2, width), f32),
            pltpu.VMEM((2, width), f32),
            pltpu.VMEM((5, rows + 8, LANES), f32),
            pltpu.VMEM((groups, rows, LANES), f32),
            pltpu.VMEM((groups, order, LANES), f32),
            pltpu.VMEM((groups, order, LANES), f32),
            pltpu.VMEM((groups, order, SUBS, LANES), f32),
            pltpu.VMEM((rows, LANES), f32),
            pltpu.VMEM((groups, order, LANES), f32),
            pltpu.VMEM((per, n, order, LANES), f32),
            pltpu.VMEM((per, n, order, LANES), f32),
            pltpu.VMEM((per, n, order, LANES), f32),
            pltpu.VMEM((rows, channels), bf16),
            copies((7,)),
            copies,
            copies,
            copies((per, n)),
            copies((per, n)),
            copies((per, n)),
            copies((per, n)),
            copies((groups,)),
            copies((groups,)),
        ],
        compiler_params=pltpu.CompilerParams(
            collective_id=0, has_side_effects=True, vmem_limit_bytes=60 * 1024 * 1024
        ),
        name="mixer",
    )(features, short_taps.swapaxes(0, 1), decays[0].T, residues[0].T, skip_gain)


def solution(mesh):
    in_specs = (
        P("pipe", "ctx", None),
        P("pipe", None, None),
        P("pipe", None, None),
        P("pipe", None, None),
        P("pipe", None),
    )
    out_specs = P("pipe", "ctx", None)
    body = functools.partial(local, mesh.shape["ctx"], mesh.shape["pipe"])
    return jax.shard_map(body, mesh=mesh, in_specs=in_specs, out_specs=out_specs, check_vma=False)
```

```python
import functools

import jax
import jax.numpy as jnp
from jax import lax
from jax.experimental import pallas as pl
from jax.experimental.pallas import tpu as pltpu
from jax.sharding import PartitionSpec as P

LANES = 128
SUBS = 8
MESH = pl.DeviceIdType.MESH


def lanes_of(group):
    return pl.ds(pl.multiple_of(group * LANES, LANES), LANES)


def mixer_kernel(
    n,
    stages,
    feat,
    taps_h,
    dec_h,
    res_h,
    skip_h,
    out,
    taps,
    dec,
    res,
    skip,
    fv,
    tail,
    halo_s,
    halo_r,
    pad,
    kv,
    drift,
    amp,
    sub_state,
    conv,
    ends,
    ends_r,
    starts,
    starts_r,
    gate,
    load_sem,
    halo_send,
    halo_recv,
    ends_send,
    ends_recv,
    starts_send,
    starts_recv,
    gate_send,
    gate_recv,
):
    rows, width = fv.shape
    channels = width // 3
    groups = channels // LANES
    per = groups // n
    order = dec.shape[0]
    sub = rows // SUBS
    me = lax.axis_index("ctx")
    stage = lax.axis_index("pipe")
    later = lax.rem(stage + 1, stages)
    before = lax.rem(stage + stages - 1, stages)

    tail_load = pltpu.make_async_copy(feat.at[0, pl.ds(rows - 16, 16)], tail, load_sem.at[0])
    kv_load = pltpu.make_async_copy(
        feat.at[0, :, pl.ds(channels, 2 * channels)],
        fv.at[:, pl.ds(channels, 2 * channels)],
        load_sem.at[1],
    )
    query_load = pltpu.make_async_copy(
        feat.at[0, :, pl.ds(0, channels)], fv.at[:, pl.ds(0, channels)], load_sem.at[2]
    )
    small_loads = [
        pltpu.make_async_copy(source, target, load_sem.at[3 + i])
        for i, (source, target) in enumerate(
            ((taps_h, taps), (dec_h, dec), (res_h, res), (skip_h, skip))
        )
    ]
    tail_load.start()
    for load in small_loads:
        load.start()
    kv_load.start()
    query_load.start()

    barrier = pltpu.get_barrier_semaphore()
    for other in (later, before):
        pl.semaphore_signal(barrier, inc=1, device_id={"pipe": other}, device_id_type=MESH)
    for step in range(1, n):
        other = lax.rem(me + step, n)
        pl.semaphore_signal(barrier, inc=1, device_id={"ctx": other}, device_id_type=MESH)

    pad[0, pl.ds(0, 8), :] = jnp.zeros((8, LANES), jnp.float32)
    pad[1, pl.ds(0, 8), :] = jnp.zeros((8, LANES), jnp.float32)
    tail_load.wait()

    @pl.loop(0, width // LANES, unroll=8)
    def _(group):
        at = lanes_of(group)
        halo_s[:, at] = tail[:, at].astype(jnp.float32)[14:16]

    pl.semaphore_wait(barrier, n + 1)

    halo_copy = pltpu.make_async_remote_copy(
        src_ref=halo_s,
        dst_ref=halo_r,
        send_sem=halo_send,
        recv_sem=halo_recv,
        device_id={"ctx": lax.rem(me + 1, n)},
        device_id_type=MESH,
    )

    @pl.when(me < n - 1)
    def _():
        halo_copy.start()

    @pl.when(me == 0)
    def _():
        halo_r[...] = jnp.zeros_like(halo_r)

    for load in small_loads:
        load.wait()
    kv_load.wait()

    place = lax.broadcasted_iota(jnp.int32, (SUBS, LANES), 0)
    place_f = place.astype(jnp.float32)

    def filtered_whole(group, slot):
        at = lanes_of(group)
        now = fv[:, at].astype(jnp.float32)
        pad[slot, pl.ds(8, rows), :] = now
        total = taps[0, :, at] * now
        for shift in range(1, 3):
            total = total + taps[shift, :, at] * pad[slot, pl.ds(8 - shift, rows), :]
        return total

    def filtered_head(group):
        at = lanes_of(group)
        now = fv[pl.ds(0, 16), at].astype(jnp.float32)[0:8]
        older = spread(halo_r[0:1, at])
        newer = spread(halo_r[1:2, at])
        one_back = jnp.where(place == 0, newer, pltpu.roll(now, 1, 0))
        two_back = jnp.where(place == 1, newer, pltpu.roll(now, 2, 0))
        two_back = jnp.where(place == 0, older, two_back)
        return taps[0, :, at] * now + taps[1, :, at] * one_back + taps[2, :, at] * two_back

    def rounded(product):
        return product.astype(jnp.bfloat16).astype(jnp.float32)

    def spread(row):
        return jnp.broadcast_to(row, (SUBS, LANES))

    def first_pass(group):
        keys = filtered_whole(groups + group, 0)
        values = filtered_whole(2 * groups + group, 1)
        kv[group] = rounded(keys * values)
        a = dec[:, lanes_of(group)]
        amp[group] = res[:, lanes_of(group)] * jnp.sqrt(a)
        one = jnp.exp(-a)
        jumps = [jnp.exp(-a * float(sub * hop)) for hop in (1, 2, 4)]
        signal = [kv[group, pl.ds(j, SUBS, stride=sub), :] for j in range(sub)]
        for m in range(order):
            lam = spread(one[m : m + 1])
            state = signal[0]
            for j in range(1, sub):
                state = state * lam + signal[j]
            for hop, jump in zip((1, 2, 4), jumps):
                factor = jnp.where(place >= hop, spread(jump[m : m + 1]), 0.0)
                state = state + factor * pltpu.roll(state, hop, 0)
            sub_state[group, m] = state
            ends[group, m : m + 1, :] = state[SUBS - 1 : SUBS]

    def join_halo(group):
        product = filtered_head(groups + group) * filtered_head(2 * groups + group)
        true = rounded(product)
        delta = true - kv[group, pl.ds(0, 8), :]
        kv[group, pl.ds(0, 8), :] = true
        a = dec[:, lanes_of(group)]
        extra = jnp.exp(a) * delta[0:1] + jnp.exp(2.0 * a) * delta[1:2]
        drift[group] = extra
        ends[group] = ends[group] + jnp.exp(-a * float(rows)) * extra

    def ends_copy(turn, owner, slot):
        return pltpu.make_async_remote_copy(
            src_ref=ends.at[owner * per + turn],
            dst_ref=ends_r.at[turn, slot],
            send_sem=ends_send.at[turn, owner],
            recv_sem=ends_recv.at[turn, slot],
            device_id={"ctx": owner},
            device_id_type=MESH,
        )

    def starts_copy(turn, target, slot):
        return pltpu.make_async_remote_copy(
            src_ref=starts.at[turn, target],
            dst_ref=starts_r.at[turn, slot],
            send_sem=starts_send.at[turn, target],
            recv_sem=starts_recv.at[turn, slot],
            device_id={"ctx": target},
            device_id_type=MESH,
        )

    def gate_copy(group):
        at = lanes_of(group)
        return pltpu.make_async_remote_copy(
            src_ref=gate.at[:, at],
            dst_ref=out.at[0, :, at],
            send_sem=gate_send.at[group],
            recv_sem=gate_recv.at[group],
            device_id={"pipe": later},
            device_id_type=MESH,
        )

    def second_pass(turn, chunk):
        group = chunk * per + turn
        entering = starts_r[turn, chunk]
        a = dec[:, lanes_of(group)]
        w = amp[group]
        one = jnp.exp(-a)
        joined = entering + drift[group]
        lam = [spread(one[m : m + 1]) for m in range(order)]
        state = []
        for m in range(order):
            decayed = jnp.exp(-spread(a[m : m + 1]) * (place_f * float(sub)))
            inner = pltpu.roll(sub_state[group, m], 1, 0) + decayed * spread(joined[m : m + 1])
            state.append(jnp.where(place >= 1, inner, spread(entering[m : m + 1])))
        gain = skip[:, lanes_of(group)]
        for j in range(sub):
            now = kv[group, pl.ds(j, SUBS, stride=sub), :]
            parts = [gain * now, None]
            for m in range(order):
                state[m] = state[m] * lam[m] + now
                term = spread(w[m : m + 1]) * state[m]
                parts[m % 2] = term if parts[m % 2] is None else parts[m % 2] + term
            conv[pl.ds(j, SUBS, stride=sub), :] = parts[0] + parts[1]
        mixed = rounded(conv[...])
        pad[2, pl.ds(6, 2), :] = halo_r[:, lanes_of(group)]
        queries = filtered_whole(group, 2)
        gate[:, lanes_of(group)] = (queries * mixed).astype(jnp.bfloat16)

    def collect(turn):
        @pl.loop(1, n + 1)
        def _(step):
            first_pass(lax.rem(me + step, n) * per + turn)

        @pl.when((turn == 0) & (me > 0))
        def _():
            halo_copy.wait_recv()

        @pl.loop(1, n + 1)
        def _(step):
            owner = lax.rem(me + step, n)
            join_halo(owner * per + turn)

            @pl.when(step < n)
            def _():
                ends_copy(turn, owner, me).start()

        ends_r[turn, me] = ends[me * per + turn]

    def scan(turn):
        @pl.loop(1, n)
        def _(step):
            other = lax.rem(me + step, n)
            ends_copy(turn, other, other).wait_recv()

        across = jnp.exp(-dec[:, lanes_of(me * per + turn)] * float(rows))

        def advance(i, state):
            starts[turn, i] = state
            return state * across + ends_r[turn, i]

        lax.fori_loop(0, n, advance, jnp.zeros((order, LANES), jnp.float32))
        starts_r[turn, me] = starts[turn, me]

        @pl.loop(1, n)
        def _(step):
            starts_copy(turn, lax.rem(me + step, n), me).start()

    def produce(turn):
        @pl.when(turn == 0)
        def _():
            query_load.wait()

        @pl.loop(0, n)
        def _(step):
            chunk = lax.rem(me + step, n)

            @pl.when(step > 0)
            def _():
                starts_copy(turn, chunk, chunk).wait_recv()

            second_pass(turn, chunk)
            gate_copy(chunk * per + turn).start()

    @pl.loop(0, per + 2)
    def _(phase):
        @pl.when(phase < per)
        def _():
            collect(phase)

        @pl.when((phase >= 1) & (phase <= per))
        def _():
            scan(phase - 1)

        @pl.when(phase >= 2)
        def _():
            produce(phase - 2)

    @pl.when(me < n - 1)
    def _():
        halo_copy.wait_send()

    @pl.loop(0, per)
    def _(turn):
        @pl.loop(1, n)
        def _(step):
            other = lax.rem(me + step, n)
            ends_copy(turn, other, me).wait_send()
            starts_copy(turn, other, me).wait_send()

    @pl.loop(0, groups)
    def _(group):
        copy = gate_copy(group)
        copy.wait_send()
        copy.wait_recv()


def local(n, stages, features, short_taps, decays, residues, skip_gain):
    rows, width = features.shape[1:]
    channels = width // 3
    order = decays.shape[2]
    groups = channels // LANES
    per = groups // n
    f32 = jnp.float32
    hbm = pl.BlockSpec(memory_space=pltpu.HBM)
    where = pl.BlockSpec(memory_space=pl.ANY)
    bf16 = jnp.bfloat16
    copies = pltpu.SemaphoreType.DMA
    return pl.pallas_call(
        functools.partial(mixer_kernel, n, stages),
        out_shape=jax.ShapeDtypeStruct((1, rows, channels), jnp.bfloat16),
        in_specs=[hbm] * 5,
        out_specs=where,
        scratch_shapes=[
            pltpu.VMEM((3, 1, width), f32),
            pltpu.VMEM((order, channels), f32),
            pltpu.VMEM((order, channels), f32),
            pltpu.VMEM((1, channels), f32),
            pltpu.VMEM((rows, width), bf16),
            pltpu.VMEM((16, width), bf16),
            pltpu.VMEM((2, width), f32),
            pltpu.VMEM((2, width), f32),
            pltpu.VMEM((3, rows + 8, LANES), f32),
            pltpu.VMEM((groups, rows, LANES), f32),
            pltpu.VMEM((groups, order, LANES), f32),
            pltpu.VMEM((groups, order, LANES), f32),
            pltpu.VMEM((groups, order, SUBS, LANES), f32),
            pltpu.VMEM((rows, LANES), f32),
            pltpu.VMEM((groups, order, LANES), f32),
            pltpu.VMEM((per, n, order, LANES), f32),
            pltpu.VMEM((per, n, order, LANES), f32),
            pltpu.VMEM((per, n, order, LANES), f32),
            pltpu.VMEM((rows, channels), bf16),
            copies((7,)),
            copies,
            copies,
            copies((per, n)),
            copies((per, n)),
            copies((per, n)),
            copies((per, n)),
            copies((groups,)),
            copies((groups,)),
        ],
        compiler_params=pltpu.CompilerParams(
            collective_id=0, has_side_effects=True, vmem_limit_bytes=48 * 1024 * 1024
        ),
        name="mixer",
    )(*[pltpu.with_memory_space_constraint(x, pltpu.HBM) for x in (features, short_taps.swapaxes(0, 1), decays[0].T, residues[0].T, skip_gain)])


def solution(mesh):
    in_specs = (
        P("pipe", "ctx", None),
        P("pipe", None, None),
        P("pipe", None, None),
        P("pipe", None, None),
        P("pipe", None),
    )
    out_specs = P("pipe", "ctx", None)
    body = functools.partial(local, mesh.shape["ctx"], mesh.shape["pipe"])
    return jax.shard_map(body, mesh=mesh, in_specs=in_specs, out_specs=out_specs, check_vma=False)
```

```python
import functools

import jax
import jax.numpy as jnp
from jax import lax
from jax.experimental import pallas as pl
from jax.experimental.pallas import tpu as pltpu
from jax.sharding import PartitionSpec as P

LANES = 128
SUBS = 8
MESH = pl.DeviceIdType.MESH


def lanes_of(group):
    return pl.ds(pl.multiple_of(group * LANES, LANES), LANES)


def mixer_kernel(
    n,
    stages,
    feat,
    taps_h,
    dec_h,
    res_h,
    skip_h,
    out,
    taps,
    dec,
    res,
    skip,
    fv,
    tail,
    halo_s,
    halo_r,
    pad,
    kv,
    drift,
    amp,
    sub_state,
    conv,
    ends,
    ends_r,
    starts,
    starts_r,
    gate,
    load_sem,
    halo_send,
    halo_recv,
    ends_send,
    ends_recv,
    starts_send,
    starts_recv,
    gate_send,
    gate_recv,
):
    rows, width = fv.shape
    channels = width // 3
    groups = channels // LANES
    per = groups // n
    order = dec.shape[0]
    sub = rows // SUBS
    me = lax.axis_index("ctx")
    stage = lax.axis_index("pipe")
    later = lax.rem(stage + 1, stages)
    before = lax.rem(stage + stages - 1, stages)

    tail_load = pltpu.make_async_copy(feat.at[0, pl.ds(rows - 16, 16)], tail, load_sem.at[0])
    kv_load = pltpu.make_async_copy(
        feat.at[0, :, pl.ds(channels, 2 * channels)],
        fv.at[:, pl.ds(channels, 2 * channels)],
        load_sem.at[1],
    )
    query_load = pltpu.make_async_copy(
        feat.at[0, :, pl.ds(0, channels)], fv.at[:, pl.ds(0, channels)], load_sem.at[2]
    )
    small_loads = [
        pltpu.make_async_copy(source, target, load_sem.at[3 + i])
        for i, (source, target) in enumerate(
            ((taps_h, taps), (dec_h, dec), (res_h, res), (skip_h, skip))
        )
    ]
    tail_load.start()
    for load in small_loads:
        load.start()
    kv_load.start()
    query_load.start()

    barrier = pltpu.get_barrier_semaphore()
    for other in (later, before):
        pl.semaphore_signal(barrier, inc=1, device_id={"pipe": other}, device_id_type=MESH)
    for step in range(1, n):
        other = lax.rem(me + step, n)
        pl.semaphore_signal(barrier, inc=1, device_id={"ctx": other}, device_id_type=MESH)

    pad[0, pl.ds(0, 8), :] = jnp.zeros((8, LANES), jnp.float32)
    pad[1, pl.ds(0, 8), :] = jnp.zeros((8, LANES), jnp.float32)
    tail_load.wait()

    @pl.loop(0, width // LANES, unroll=8)
    def _(group):
        at = lanes_of(group)
        halo_s[:, at] = tail[:, at].astype(jnp.float32)[14:16]

    pl.semaphore_wait(barrier, n + 1)

    halo_copy = pltpu.make_async_remote_copy(
        src_ref=halo_s,
        dst_ref=halo_r,
        send_sem=halo_send,
        recv_sem=halo_recv,
        device_id={"ctx": lax.rem(me + 1, n)},
        device_id_type=MESH,
    )

    @pl.when(me < n - 1)
    def _():
        halo_copy.start()

    @pl.when(me == 0)
    def _():
        halo_r[...] = jnp.zeros_like(halo_r)

    for load in small_loads:
        load.wait()
    kv_load.wait()

    place = lax.broadcasted_iota(jnp.int32, (SUBS, LANES), 0)
    place_f = place.astype(jnp.float32)

    def filtered_whole(group, slot):
        at = lanes_of(group)
        now = fv[:, at].astype(jnp.float32)
        pad[slot, pl.ds(8, rows), :] = now
        total = taps[0, :, at] * now
        for shift in range(1, 3):
            total = total + taps[shift, :, at] * pad[slot, pl.ds(8 - shift, rows), :]
        return total

    def filtered_head(group):
        at = lanes_of(group)
        now = fv[pl.ds(0, 16), at].astype(jnp.float32)[0:8]
        older = spread(halo_r[0:1, at])
        newer = spread(halo_r[1:2, at])
        one_back = jnp.where(place == 0, newer, pltpu.roll(now, 1, 0))
        two_back = jnp.where(place == 1, newer, pltpu.roll(now, 2, 0))
        two_back = jnp.where(place == 0, older, two_back)
        return taps[0, :, at] * now + taps[1, :, at] * one_back + taps[2, :, at] * two_back

    def rounded(product):
        return product.astype(jnp.bfloat16).astype(jnp.float32)

    def spread(row):
        return jnp.broadcast_to(row, (SUBS, LANES))

    def first_pass(group):
        keys = filtered_whole(groups + group, 0)
        values = filtered_whole(2 * groups + group, 1)
        kv[group] = rounded(keys * values)
        a = dec[:, lanes_of(group)]
        amp[group] = res[:, lanes_of(group)] * jnp.sqrt(a)
        one = jnp.exp(-a)
        jumps = [jnp.exp(-a * float(sub * hop)) for hop in (1, 2, 4)]
        signal = [kv[group, pl.ds(j, SUBS, stride=sub), :] for j in range(sub)]
        for m in range(order):
            lam = spread(one[m : m + 1])
            state = signal[0]
            for j in range(1, sub):
                state = state * lam + signal[j]
            for hop, jump in zip((1, 2, 4), jumps):
                factor = jnp.where(place >= hop, spread(jump[m : m + 1]), 0.0)
                state = state + factor * pltpu.roll(state, hop, 0)
            sub_state[group, m] = state
            ends[group, m : m + 1, :] = state[SUBS - 1 : SUBS]

    def join_halo(group):
        product = filtered_head(groups + group) * filtered_head(2 * groups + group)
        true = rounded(product)
        delta = true - kv[group, pl.ds(0, 8), :]
        kv[group, pl.ds(0, 8), :] = true
        a = dec[:, lanes_of(group)]
        extra = jnp.exp(a) * delta[0:1] + jnp.exp(2.0 * a) * delta[1:2]
        drift[group] = extra
        ends[group] = ends[group] + jnp.exp(-a * float(rows)) * extra

    def ends_copy(turn, owner, slot):
        return pltpu.make_async_remote_copy(
            src_ref=ends.at[owner * per + turn],
            dst_ref=ends_r.at[turn, slot],
            send_sem=ends_send.at[turn, owner],
            recv_sem=ends_recv.at[turn, slot],
            device_id={"ctx": owner},
            device_id_type=MESH,
        )

    def starts_copy(turn, target, slot):
        return pltpu.make_async_remote_copy(
            src_ref=starts.at[turn, target],
            dst_ref=starts_r.at[turn, slot],
            send_sem=starts_send.at[turn, target],
            recv_sem=starts_recv.at[turn, slot],
            device_id={"ctx": target},
            device_id_type=MESH,
        )

    def gate_copy(group):
        at = lanes_of(group)
        return pltpu.make_async_remote_copy(
            src_ref=gate.at[:, at],
            dst_ref=out.at[0, :, at],
            send_sem=gate_send.at[group],
            recv_sem=gate_recv.at[group],
            device_id={"pipe": later},
            device_id_type=MESH,
        )

    def second_pass(turn, chunk):
        group = chunk * per + turn
        entering = starts_r[turn, chunk]
        a = dec[:, lanes_of(group)]
        w = amp[group]
        one = jnp.exp(-a)
        joined = entering + drift[group]
        lam = [spread(one[m : m + 1]) for m in range(order)]
        state = []
        for m in range(order):
            decayed = jnp.exp(-spread(a[m : m + 1]) * (place_f * float(sub)))
            inner = pltpu.roll(sub_state[group, m], 1, 0) + decayed * spread(joined[m : m + 1])
            state.append(jnp.where(place >= 1, inner, spread(entering[m : m + 1])))
        gain = skip[:, lanes_of(group)]
        for j in range(sub):
            now = kv[group, pl.ds(j, SUBS, stride=sub), :]
            parts = [gain * now, None]
            for m in range(order):
                state[m] = state[m] * lam[m] + now
                term = spread(w[m : m + 1]) * state[m]
                parts[m % 2] = term if parts[m % 2] is None else parts[m % 2] + term
            conv[pl.ds(j, SUBS, stride=sub), :] = parts[0] + parts[1]
        mixed = rounded(conv[...])
        pad[2, pl.ds(6, 2), :] = halo_r[:, lanes_of(group)]
        queries = filtered_whole(group, 2)
        gate[:, lanes_of(group)] = (queries * mixed).astype(jnp.bfloat16)

    def collect(turn):
        @pl.loop(1, n + 1)
        def _(step):
            first_pass(lax.rem(me + step, n) * per + turn)

        @pl.when((turn == 0) & (me > 0))
        def _():
            halo_copy.wait_recv()

        @pl.loop(1, n + 1)
        def _(step):
            owner = lax.rem(me + step, n)
            join_halo(owner * per + turn)

            @pl.when(step < n)
            def _():
                ends_copy(turn, owner, me).start()

        ends_r[turn, me] = ends[me * per + turn]

    def scan(turn):
        @pl.loop(1, n)
        def _(step):
            other = lax.rem(me + step, n)
            ends_copy(turn, other, other).wait_recv()

        across = jnp.exp(-dec[:, lanes_of(me * per + turn)] * float(rows))

        def advance(i, state):
            starts[turn, i] = state
            return state * across + ends_r[turn, i]

        lax.fori_loop(0, n, advance, jnp.zeros((order, LANES), jnp.float32))
        starts_r[turn, me] = starts[turn, me]

        @pl.loop(1, n)
        def _(step):
            starts_copy(turn, lax.rem(me + step, n), me).start()

    def produce(turn):
        @pl.when(turn == 0)
        def _():
            query_load.wait()

        @pl.loop(0, n)
        def _(step):
            chunk = lax.rem(me + step, n)

            @pl.when(step > 0)
            def _():
                starts_copy(turn, chunk, chunk).wait_recv()

            second_pass(turn, chunk)
            gate_copy(chunk * per + turn).start()

    @pl.loop(0, per + 2)
    def _(phase):
        @pl.when(phase < per)
        def _():
            collect(phase)

        @pl.when(phase >= 2)
        def _():
            produce(phase - 2)

        @pl.when((phase >= 1) & (phase <= per))
        def _():
            scan(phase - 1)

    @pl.when(me < n - 1)
    def _():
        halo_copy.wait_send()

    @pl.loop(0, per)
    def _(turn):
        @pl.loop(1, n)
        def _(step):
            other = lax.rem(me + step, n)
            ends_copy(turn, other, me).wait_send()
            starts_copy(turn, other, me).wait_send()

    @pl.loop(0, groups)
    def _(group):
        copy = gate_copy(group)
        copy.wait_send()
        copy.wait_recv()


def local(n, stages, features, short_taps, decays, residues, skip_gain):
    rows, width = features.shape[1:]
    channels = width // 3
    order = decays.shape[2]
    groups = channels // LANES
    per = groups // n
    f32 = jnp.float32
    hbm = pl.BlockSpec(memory_space=pltpu.HBM)
    where = pl.BlockSpec(memory_space=pl.ANY)
    bf16 = jnp.bfloat16
    copies = pltpu.SemaphoreType.DMA
    return pl.pallas_call(
        functools.partial(mixer_kernel, n, stages),
        out_shape=jax.ShapeDtypeStruct((1, rows, channels), jnp.bfloat16),
        in_specs=[hbm] * 5,
        out_specs=where,
        scratch_shapes=[
            pltpu.VMEM((3, 1, width), f32),
            pltpu.VMEM((order, channels), f32),
            pltpu.VMEM((order, channels), f32),
            pltpu.VMEM((1, channels), f32),
            pltpu.VMEM((rows, width), bf16),
            pltpu.VMEM((16, width), bf16),
            pltpu.VMEM((2, width), f32),
            pltpu.VMEM((2, width), f32),
            pltpu.VMEM((3, rows + 8, LANES), f32),
            pltpu.VMEM((groups, rows, LANES), f32),
            pltpu.VMEM((groups, order, LANES), f32),
            pltpu.VMEM((groups, order, LANES), f32),
            pltpu.VMEM((groups, order, SUBS, LANES), f32),
            pltpu.VMEM((rows, LANES), f32),
            pltpu.VMEM((groups, order, LANES), f32),
            pltpu.VMEM((per, n, order, LANES), f32),
            pltpu.VMEM((per, n, order, LANES), f32),
            pltpu.VMEM((per, n, order, LANES), f32),
            pltpu.VMEM((rows, channels), bf16),
            copies((7,)),
            copies,
            copies,
            copies((per, n)),
            copies((per, n)),
            copies((per, n)),
            copies((per, n)),
            copies((groups,)),
            copies((groups,)),
        ],
        compiler_params=pltpu.CompilerParams(
            collective_id=0, has_side_effects=True, vmem_limit_bytes=48 * 1024 * 1024
        ),
        name="mixer",
    )(*[pltpu.with_memory_space_constraint(x, pltpu.HBM) for x in (features, short_taps.swapaxes(0, 1), decays[0].T, residues[0].T, skip_gain)])


def solution(mesh):
    in_specs = (
        P("pipe", "ctx", None),
        P("pipe", None, None),
        P("pipe", None, None),
        P("pipe", None, None),
        P("pipe", None),
    )
    out_specs = P("pipe", "ctx", None)
    body = functools.partial(local, mesh.shape["ctx"], mesh.shape["pipe"])
    return jax.shard_map(body, mesh=mesh, in_specs=in_specs, out_specs=out_specs, check_vma=False)
```
